32 devices in a mesh: leaf: 4 (over y, x), row: 4 (over z), col: 2 (over core).
Axes of the slice: x: 2, y: 2, z: 4, core: 2. Of those that a mesh axis runs over, the one named last changes fastest.
Arguments:
- contribution: float32 [4, 10, 4, 128, 40, 2, 128], P('leaf', None, 'row', None, None, 'col'), may hold values from -6 to 6
- panel_left: float32 [4, 10, 4, 128, 2048], P('leaf', None, 'row', None, 'col'), may hold values from -0.1875 to 0.1875
- panel_right: float32 [4, 1024, 40, 2, 128], P('leaf', 'row', None, 'col'), may hold values from -6 to 6
- block_masks: int32 [4, 2, 40, 40], replicated, may hold values 0 or 1
- index_maps: int32 [4, 2, 40], replicated, may hold values from 0 to 63, as said below
- pivot_diag: float32 [512], replicated, may hold values from 80 to 160
Outputs:
- front: float32 [4, 16, 4, 128, 32, 2, 128], P('leaf', None, 'row', None, None, 'col')
The draws below stay inside these ranges and needn't reach their ends.
Inputs may be any that keep to these rules, and one draw needn't show every extreme that they name: For each child, index_maps[l, s] is one-to-one, and index_maps[l, s, a] is congruent to a modulo 4.
All inputs are finite; a program needn't handle non-finite values.
Results may differ from the reference program's by a relative error of at most 0.0001.
Values sent between devices are 32-bit elements; how exact they have to be, the bound alone decides.
A program may use at most 256 MiB of HBM per device.

```python
import math
import jax
import jax.numpy as jnp
from jax import lax

BS = 128
CB = 40
PB = 64
PANB = 4
CPAN = 1024
NS_STEPS = 2
RES = 4
N_LEAF = 4
N_ROW = 4
N_COL = 2


def draw_index_maps(key, part):
    per_class = CB // RES
    pool = PB // RES
    keys = jax.random.split(key, N_LEAF * 2 * RES)
    shuffled = jax.vmap(lambda single: jax.random.permutation(single, pool))(keys)[:, :per_class]
    shuffled = shuffled.reshape(N_LEAF, 2, RES, per_class).astype(jnp.int32)
    residue = jnp.arange(RES, dtype=jnp.int32)[None, None, :, None]
    values = residue + RES * shuffled
    return jnp.transpose(values, (0, 1, 3, 2)).reshape(N_LEAF, 2, CB).astype(jnp.int32)


def plant(values, rng, least, top_value):
    extent = values.shape
    index_at = [jax.random.randint(jax.random.fold_in(rng, axis), (), 0, extent[axis]) for axis in range(len(extent))]
    values = values.at[tuple(index_at)].set(least)
    longest = extent.index(max(extent))
    index_at[longest] = (index_at[longest] + 1) % extent[longest]
    return values.at[tuple(index_at)].set(top_value)


def levels(own_key, dims, cuts, least, top_value):
    def one(dim, blocks):
        steps = jax.random.uniform(jax.random.fold_in(jax.random.fold_in(own_key, 6), dim), (blocks,), jnp.float32, least / len(cuts), top_value / len(cuts))
        return jnp.repeat(jnp.exp(steps), dims[dim] // blocks).reshape((-1,) + (1,) * (len(dims) - dim - 1))

    gain = one(*cuts[0])
    for cut in cuts[1:]:
        gain = gain * one(*cut)
    return gain


def centred(own_key, dims, scale, bound, pieces=(), kind=jnp.bfloat16):
    values = jax.random.normal(own_key, dims, jnp.float32) * scale
    if len(pieces) > 0:
        values = levels(own_key, dims, pieces, -0.22, 0.18) * values
    return jnp.clip(values, min=-bound, max=bound).astype(kind)


def setup_inputs(seed: int = 0) -> dict:
    splits = jax.random.split(jax.random.key(seed), 7)
    contribution = centred(splits[0], (N_LEAF, CB // N_ROW, N_ROW, BS, CB // (N_COL // 2), N_COL, BS), 1.0, 6.0, ((0, 4), (2, 4), (5, 2)), jnp.float32)
    panel_left = centred(splits[1], (N_LEAF, CB // N_ROW, N_ROW, BS, 2 * CPAN), CPAN ** -0.5, 0.1875, ((0, 4), (2, 4), (4, 2)), jnp.float32)
    panel_right = centred(splits[2], (N_LEAF, CPAN, CB // (N_COL // 2), N_COL, BS), 1.0, 6.0, ((0, 4), (1, 4), (3, 2)), jnp.float32)
    block_masks = plant((jax.random.randint(splits[3], (N_LEAF, 2, CB, CB), 0, 4) < 3).astype(jnp.int32), jax.random.fold_in(splits[3], 1), 0, 1)
    index_maps = draw_index_maps(jax.random.fold_in(splits[6], 71), 0)
    pivot_diag = jnp.clip(jnp.exp(jax.random.uniform(splits[5], (PANB * BS,), jnp.float32, math.log(80.0), math.log(160.0))), 80.0, 160.0)
    return {"contribution": contribution, "panel_left": panel_left, "panel_right": panel_right, "block_masks": block_masks, "index_maps": index_maps, "pivot_diag": pivot_diag}


def child_schur(contribution, panel_left, panel_right, block_masks, source, side):
    half_cols = N_COL // 2
    order = CB * BS
    cmat = contribution[source][:, :, :, :, side * half_cols:(side + 1) * half_cols, :].reshape(order, order)
    left = panel_left[source].reshape(CB // N_ROW, N_ROW, BS, CPAN, 2)[:, :, :, :, side].reshape(order, CPAN)
    right = panel_right[source][:, :, side * half_cols:(side + 1) * half_cols, :].reshape(CPAN, order)
    schur = cmat - jnp.dot(left, right, precision=lax.Precision.HIGHEST, preferred_element_type=jnp.float32)
    masking = block_masks[source, side].astype(jnp.float32)
    return schur.reshape(CB, BS, CB, BS) * masking[:, None, :, None]


def reference(contribution, panel_left, panel_right, block_masks, index_maps, pivot_diag):
    width = PANB * BS
    fronts = []
    for leaf_index in range(N_LEAF):
        total = jnp.zeros((PB, BS, PB, BS), jnp.float32)
        for source, side in ((leaf_index, 0), (leaf_index ^ 1, 1)):
            schur = child_schur(contribution, panel_left, panel_right, block_masks, source, side)
            mapping = index_maps[source, side].astype(jnp.int32)
            spread = jnp.zeros((PB, BS, CB, BS), jnp.float32).at[mapping].add(schur)
            total = total + jnp.zeros((PB, BS, PB, BS), jnp.float32).at[:, :, mapping].add(spread)
        matrix = total.reshape(PB * BS, PB * BS)
        diagonal = jnp.arange(width)
        matrix = matrix.at[diagonal, diagonal].add(pivot_diag)
        pivot = matrix[:width, :width]
        inverse = jnp.diag(1.0 / pivot_diag)
        for sweep in range(NS_STEPS):
            middle = jnp.dot(inverse, pivot, precision=lax.Precision.HIGHEST, preferred_element_type=jnp.float32)
            inverse = 2.0 * inverse - jnp.dot(middle, inverse, precision=lax.Precision.HIGHEST, preferred_element_type=jnp.float32)
        inside = jnp.arange(PB * BS) < width
        western = jnp.where(inside[:, None], 0.0, matrix[:, :width])
        northern = jnp.where(inside[None, :], 0.0, matrix[:width, :])
        scaled = jnp.dot(western, inverse, precision=lax.Precision.HIGHEST, preferred_element_type=jnp.float32)
        update = jnp.dot(scaled, northern, precision=lax.Precision.HIGHEST, preferred_element_type=jnp.float32)
        result = jnp.where(inside[:, None] | inside[None, :], 0.0, matrix - update)
        fronts.append(result.reshape(PB // N_ROW, N_ROW, BS, PB // N_COL, N_COL, BS))
    return jnp.stack(fronts)
```

```python
import functools

import jax
import jax.numpy as jnp
from jax import lax
from jax.experimental import pallas as pl
from jax.experimental.pallas import tpu as pltpu
from jax.sharding import PartitionSpec as P

BS = 128
CB = 40
PB = 64
PANB = 4
CPAN = 1024
NS_STEPS = 2


def partner(block, axis, stride):
    count = lax.axis_size(axis)
    route = []
    for low in range(count):
        high = low | 1 << stride
        if high != low and high < count:
            route += [(low, high), (high, low)]
    return lax.ppermute(block, axis, route)


def from_root(x, axis, root):
    mine = lax.axis_index(axis) == root
    return lax.psum(jnp.where(mine, x, jnp.zeros_like(x)), axis)


def matmul(first, second):
    return jnp.dot(
        first, second, precision=lax.Precision.HIGHEST, preferred_element_type=jnp.float32
    )


def on_device_general(contribution, panel_left, panel_right, block_masks, index_maps, pivot_diag):
    row_count = lax.axis_size("row")
    col_count = lax.axis_size("col")
    half_cols = col_count // 2
    leaf_index = lax.axis_index("leaf")
    row_index = lax.axis_index("row")
    col_index = lax.axis_index("col")
    child_side = col_index // half_cols
    group_index = col_index % half_cols
    child_rows = contribution.shape[1]
    child_cols = contribution.shape[4]
    parent_rows = PB // row_count
    parent_cols = PB // col_count
    width = PANB * BS
    cmat = contribution.reshape(child_rows * BS, child_cols * BS)
    gathered_right = lax.all_gather(panel_right, "row", axis=1, tiled=True)
    right = gathered_right.reshape(CPAN, child_cols * BS)
    gathered_left = lax.all_gather(panel_left, "col", axis=4, tiled=True)
    paired = gathered_left.reshape(child_rows * BS, CPAN, 2)
    first_child = paired[:, :, 0]
    second_child = paired[:, :, 1]
    left = jnp.where(child_side == 0, first_child, second_child)
    product = matmul(left, right)
    own_mask = block_masks[leaf_index, child_side]
    own_mask = own_mask.reshape(child_rows, row_count, CB)[:, row_index]
    own_mask = own_mask.reshape(child_rows, child_cols, half_cols)[:, :, group_index].astype(
        jnp.float32
    )
    schur = (cmat - product).reshape(child_rows, BS, child_cols, BS) * own_mask[:, None, :, None]
    own_map = index_maps[leaf_index, child_side]
    target = own_map.reshape(child_cols, half_cols)[:, group_index]
    stays = (target % col_count // half_cols == child_side).astype(jnp.float32)
    kept_here = schur * stays[None, None, :, None]
    leaving = schur * (1.0 - stays)[None, None, :, None]
    top_bit = col_count.bit_length() - 2
    arrived = partner(leaving, "col", top_bit)
    outgoing = jnp.where(child_side == 0, arrived, kept_here)
    staying = jnp.where(child_side == 0, kept_here, arrived)
    incoming = partner(outgoing, "leaf", 0)

    def assemble(piece, mapping):
        row_map = mapping.reshape(child_rows, row_count)[:, row_index] // row_count
        row_select = (row_map[None, :] == jnp.arange(parent_rows)[:, None]).astype(jnp.float32)
        col_map = mapping.reshape(child_cols, half_cols)[:, group_index]
        wanted = jnp.arange(parent_cols) * col_count + col_index
        col_select = (col_map[None, :] == wanted[:, None]).astype(jnp.float32)
        placed = jnp.einsum("pk,kxly->pxly", row_select, piece, precision=lax.Precision.HIGHEST)
        return jnp.einsum("pxly,ql->pxqy", placed, col_select, precision=lax.Precision.HIGHEST)

    first_map = index_maps[leaf_index, 0]
    second_map = index_maps[jnp.bitwise_xor(leaf_index, 1), 1]
    assembled = assemble(staying, first_map) + assemble(incoming, second_map)
    row_blocks = jnp.arange(parent_rows) * row_count + row_index
    col_blocks = jnp.arange(parent_cols) * col_count + col_index
    on_pivot = ((row_blocks[:, None] == col_blocks[None, :]) & (row_blocks[:, None] < PANB)).astype(
        jnp.float32
    )
    diag_rows = pivot_diag.reshape(PANB, BS)[jnp.clip(row_blocks, 0, PANB - 1)]
    identity = jnp.eye(BS, dtype=jnp.float32)
    assembled = assembled + on_pivot[:, None, :, None] * (
        diag_rows[:, :, None, None] * identity[None, :, None, :]
    )
    column_parts = []
    for block in range(PANB):
        owned = assembled[:, :, block // col_count, :]
        column_parts.append(from_root(owned, "col", block % col_count))
    western_raw = jnp.stack(column_parts, axis=2).reshape(parent_rows, BS, width)
    pieces_row = PANB // row_count
    north_raw = lax.all_gather(assembled[:pieces_row], "row", axis=0, tiled=True)
    north_raw = north_raw.reshape(row_count, pieces_row, BS, parent_cols * BS)
    north_raw = jnp.transpose(north_raw, (1, 0, 2, 3)).reshape(width, parent_cols * BS)
    pivot = lax.all_gather(western_raw[:pieces_row], "row", axis=0, tiled=True)
    pivot = jnp.transpose(pivot.reshape(row_count, pieces_row, BS, width), (1, 0, 2, 3)).reshape(
        width, width
    )
    inverse = jnp.diag(1.0 / pivot_diag)
    for sweep in range(NS_STEPS):
        inverse = 2.0 * inverse - matmul(matmul(inverse, pivot), inverse)
    western = (western_raw * (row_blocks >= PANB).astype(jnp.float32)[:, None, None]).reshape(
        parent_rows * BS, width
    )
    col_keep = jnp.repeat((col_blocks >= PANB).astype(jnp.float32), BS)
    northern = north_raw * col_keep[None, :]
    update = matmul(matmul(western, inverse), northern)
    result = assembled.reshape(parent_rows * BS, parent_cols * BS) - update
    keep_mask = ((row_blocks >= PANB)[:, None] & (col_blocks >= PANB)[None, :]).astype(jnp.float32)
    result = result.reshape(parent_rows, BS, parent_cols, BS) * keep_mask[:, None, :, None]
    return result.reshape(1, parent_rows, 1, BS, parent_cols, 1, BS)


GROUP = 8
VMEM_LIMIT = 60 * 1024 * 1024


def split(x):
    high = lax.reduce_precision(x, 8, 7)
    return high.astype(jnp.bfloat16), (x - high).astype(jnp.bfloat16)


def split_in_kernel(x):
    high = x.astype(jnp.bfloat16)
    return high, (x - high.astype(jnp.float32)).astype(jnp.bfloat16)


def dot3(a_high, a_low, b_high, b_low):
    dot = functools.partial(jnp.dot, preferred_element_type=jnp.float32)
    return dot(a_high, b_high) + (dot(a_high, b_low) + dot(a_low, b_high))


def schur_kernel(chunk, rows_at_once, side_ref, mask_ref, lh_ref, ll_ref, r_ref, c_ref, own_ref, send_ref):
    side = side_ref[0]
    rows, depth = lh_ref.shape
    r_flat = r_ref.reshape(depth * GROUP, BS)
    c_flat = c_ref.reshape(rows * GROUP, BS)
    for pair in range(GROUP // 2):
        q_own = 2 * pair + side
        q_send = 2 * pair + 1 - side
        right = jnp.concatenate(
            [r_flat[pl.ds(q, depth, stride=GROUP), :] for q in (q_own, q_send)], axis=1
        )
        right_high, right_low = split_in_kernel(right)

        def body(step, carry):
            start = pl.multiple_of(step * rows_at_once, rows_at_once)
            lines = pl.ds(start, rows_at_once)
            product = dot3(lh_ref[lines, :], ll_ref[lines, :], right_high, right_low)
            for place, (q, out_ref) in enumerate(((q_own, own_ref), (q_send, send_ref))):
                c_part = c_flat[pl.ds(start * GROUP + q, rows_at_once, stride=GROUP), :]
                value = c_part - product[:, place * BS : (place + 1) * BS]
                for block in range(rows_at_once // BS):
                    keep = mask_ref[step * (rows_at_once // BS) + block, chunk * GROUP + q]
                    out_ref[pair, pl.ds(start + block * BS, BS), :] = value[
                        block * BS : (block + 1) * BS
                    ] * keep.astype(jnp.float32)
            return carry

        lax.fori_loop(0, rows // rows_at_once, body, 0)


def schur_chunk(chunk, side, mask, left_high, left_low, right, cmat):
    rows, depth = left_high.shape
    half = jax.ShapeDtypeStruct((GROUP // 2, rows, BS), jnp.float32)
    whole = lambda shape: pl.BlockSpec(shape, lambda i, *_: (0,) * len(shape))
    rows_at_once = 2 * BS if rows % (2 * BS) == 0 else BS
    return pl.pallas_call(
        functools.partial(schur_kernel, chunk, rows_at_once),
        out_shape=(half, half),
        grid_spec=pltpu.PrefetchScalarGridSpec(
            num_scalar_prefetch=2,
            grid=(1,),
            in_specs=[
                whole((rows, depth)),
                whole((rows, depth)),
                whole((depth, GROUP, BS)),
                pl.BlockSpec((rows, GROUP, BS), lambda i, *_: (0, chunk, 0)),
            ],
            out_specs=[whole(half.shape), whole(half.shape)],
        ),
        compiler_params=pltpu.CompilerParams(vmem_limit_bytes=VMEM_LIMIT),
        cost_estimate=pl.CostEstimate(
            flops=6 * rows * depth * GROUP * BS,
            bytes_accessed=4 * (rows * depth + depth * GROUP * BS + 2 * rows * GROUP * BS),
            transcendentals=0,
        ),
        name="schur_chunk",
    )(side, mask, left_high, left_low, right, cmat)


def update_kernel(first_keep, panel_cols, row_step, first_col, first_colok, second_col, second_colok, first_row, first_rowok, second_row, second_rowok, *refs):
    first = refs[:GROUP]
    second = refs[GROUP : 2 * GROUP]
    wh_ref, wl_ref = refs[2 * GROUP : 2 * GROUP + 2]
    v_refs = refs[2 * GROUP + 2 : 2 * GROUP + 2 + GROUP // 2]
    out_ref = refs[-1]
    rows, width = wh_ref.shape
    out_flat = out_ref.reshape(rows * GROUP, BS)
    group = pl.program_id(0)
    blocks = row_step // BS
    for pair in range(GROUP // 2):
        v_ref = v_refs[pair]
        v = jnp.concatenate([v_ref[:, i].reshape(width, BS) for i in range(2)], axis=1)
        v_high, v_low = split_in_kernel(v)

        def body(step, carry):
            lines = pl.ds(pl.multiple_of(step * row_step, row_step), row_step)
            product = dot3(wh_ref[lines, :], wl_ref[lines, :], v_high, v_low)
            for block in range(blocks):
                k = step * blocks + block
                for i in range(2):
                    place = 2 * pair + i
                    q = group * GROUP + place
                    keep = jnp.where((k >= first_keep) & (q >= panel_cols), 1.0, 0.0).astype(
                        jnp.float32
                    )
                    total = -product[block * BS : (block + 1) * BS, i * BS : (i + 1) * BS]
                    for slabs, col_ok, row_at, row_ok in (
                        (first, first_colok, first_row, first_rowok),
                        (second, second_colok, second_row, second_rowok),
                    ):
                        use = (col_ok[q] * row_ok[k]).astype(jnp.float32)
                        from_row = pl.multiple_of(row_at[k] * BS, BS)
                        total = total + slabs[place][0, pl.ds(from_row, BS), :] * use
                    out_flat[pl.ds(k * (BS * GROUP) + place, BS, stride=GROUP), :] = total * keep
            return carry

        lax.fori_loop(0, rows // row_step, body, 0)


def update(first_keep, panel_cols, scalars, first, second, w_high, w_low, northern, parent_cols):
    rows, width = w_high.shape
    child_rows = first.shape[1]
    pieces = northern.shape[0]
    row_step = 4 * BS if rows % (4 * BS) == 0 else BS

    def slab(which, place):
        def at(g, *prefetched):
            return prefetched[which][g * GROUP + place], 0, 0

        return pl.BlockSpec((1, child_rows, BS), at)

    def north(pair):
        def at(g, *_):
            return 0, jnp.maximum(g * (GROUP // 2) + pair - panel_cols // 2, 0), 0, 0

        return pl.BlockSpec((pieces, 2, BS, BS), at)

    whole = pl.BlockSpec((rows, width), lambda g, *_: (0, 0), pipeline_mode=pl.Buffered(1))
    return pl.pallas_call(
        functools.partial(update_kernel, first_keep, panel_cols, row_step),
        out_shape=jax.ShapeDtypeStruct((rows, parent_cols, BS), jnp.float32),
        grid_spec=pltpu.PrefetchScalarGridSpec(
            num_scalar_prefetch=8,
            grid=(parent_cols // GROUP,),
            in_specs=[slab(0, i) for i in range(GROUP)]
            + [slab(2, i) for i in range(GROUP)]
            + [whole, whole]
            + [north(i) for i in range(GROUP // 2)],
            out_specs=pl.BlockSpec((rows, GROUP, BS), lambda g, *_: (0, g, 0)),
        ),
        compiler_params=pltpu.CompilerParams(vmem_limit_bytes=VMEM_LIMIT),
        cost_estimate=pl.CostEstimate(
            flops=6 * rows * width * parent_cols * BS,
            bytes_accessed=4 * (2 * child_rows + rows + width) * parent_cols * BS,
            transcendentals=0,
        ),
        name="front_update",
    )(*scalars, *([first] * GROUP), *([second] * GROUP), w_high, w_low, *([northern] * (GROUP // 2)))


def inverse_map(targets, count):
    hits = targets[None, :] == jnp.arange(count, dtype=jnp.int32)[:, None]
    return jnp.argmax(hits, axis=1).astype(jnp.int32), jnp.any(hits, axis=1).astype(jnp.int32)


def on_device_paired(contribution, panel_left, panel_right, block_masks, index_maps, pivot_diag):
    row_count = lax.axis_size("row")
    col_count = lax.axis_size("col")
    leaf_index = lax.axis_index("leaf")
    row_index = lax.axis_index("row")
    side = lax.axis_index("col")
    child_rows = contribution.shape[1]
    child_cols = contribution.shape[4]
    blocks = child_rows * row_count
    rows = child_rows * BS
    parent_rows = PB // row_count
    parent_cols = PB // col_count
    width = PANB * BS
    panel_rows = PANB // row_count
    panel_cols = PANB // col_count
    exact = lax.Precision.HIGHEST

    cmat = contribution.reshape(rows, child_cols, BS)
    right_local = panel_right.reshape(panel_right.shape[1], child_cols, BS)
    depth = right_local.shape[0] * row_count
    chunks = child_cols // GROUP

    gathered = []
    for chunk in range(chunks):
        piece = right_local[:, chunk * GROUP : (chunk + 1) * GROUP]
        if gathered:
            piece, gathered[-1] = lax.optimization_barrier((piece, gathered[-1]))
        gathered.append(lax.all_gather(piece, "row", axis=0, tiled=True))

    local_left = panel_left.reshape(rows, panel_left.shape[4])
    local_depth = local_left.shape[1] // 2
    line = jnp.arange(2 * local_depth)[:, None]
    pick = 2 * jnp.arange(local_depth)[None, :]
    kept = matmul(local_left, (line == pick + side).astype(jnp.float32))
    given = matmul(local_left, (line == pick + 1 - side).astype(jnp.float32))
    taken = partner(given, "col", 0)
    left = jnp.where(
        side == 0,
        jnp.concatenate([kept, taken], axis=1),
        jnp.concatenate([taken, kept], axis=1),
    )
    left_high, left_low = split(left)

    mask = block_masks[leaf_index, side].reshape(child_rows, row_count, blocks)[:, row_index]
    side_arg = side.astype(jnp.int32).reshape(1)
    first = jnp.zeros((child_cols // 2, rows, BS), jnp.float32)
    second = jnp.zeros((child_cols // 2, rows, BS), jnp.float32)
    for chunk in range(chunks):
        own, sent = schur_chunk(chunk, side_arg, mask, left_high, left_low, gathered[chunk], cmat)
        got = partner(sent, "col", 0)
        incoming = partner(jnp.where(side == 0, got, own), "leaf", 0)
        at = chunk * (GROUP // 2)
        first = lax.dynamic_update_slice(first, jnp.where(side == 0, own, got), (at, 0, 0))
        second = lax.dynamic_update_slice(second, incoming, (at, 0, 0))

    maps = (index_maps[leaf_index, 0], index_maps[jnp.bitwise_xor(leaf_index, 1), 1])
    row_targets = [
        m.reshape(child_rows, row_count)[:, row_index].astype(jnp.int32) // row_count for m in maps
    ]
    col_targets = [
        m.reshape(child_cols // 2, 2)[:, side].astype(jnp.int32) // col_count for m in maps
    ]
    cols = [inverse_map(t, parent_cols) for t in col_targets]
    lines = [inverse_map(t, parent_rows) for t in row_targets]
    children = (first, second)

    identity = jnp.eye(BS, dtype=jnp.float32)
    diag = pivot_diag.reshape(PANB, BS)
    col_blocks = jnp.arange(parent_cols) * col_count + side

    north_local = []
    for piece in range(panel_rows):
        strip = jnp.zeros((parent_cols, BS, BS), jnp.float32)
        for child, (at, ok), target in zip(children, lines, col_targets):
            taken_rows = lax.dynamic_slice(
                child, (0, at[piece] * BS, 0), (child.shape[0], BS, BS)
            ) * ok[piece].astype(jnp.float32)
            select = (target[None, :] == jnp.arange(parent_cols)[:, None]).astype(jnp.float32)
            strip = strip + jnp.einsum("qj,jxy->qxy", select, taken_rows, precision=exact)
        row_block = piece * row_count + row_index
        on_pivot = (col_blocks == row_block).astype(jnp.float32)
        strip = strip + on_pivot[:, None, None] * (diag[row_block][:, None] * identity)[None]
        north_local.append(strip)
    north_local = jnp.stack(north_local)

    corner = lax.all_gather(north_local[:, :panel_cols], "row", axis=1)
    trailing, corner = lax.optimization_barrier((north_local[:, panel_cols:], corner))
    northern = lax.all_gather(trailing, "row", axis=1)
    northern = northern.reshape(PANB, parent_cols - panel_cols, BS, BS)

    def both_sides(mine):
        other = partner(mine, "col", 0)
        return jnp.where(side == 0, jnp.stack([mine, other]), jnp.stack([other, mine]))

    corner = corner.reshape(PANB, panel_cols, BS, BS)
    pivot = jnp.transpose(both_sides(corner), (1, 3, 2, 0, 4)).reshape(width, width)

    west = jnp.zeros((panel_cols, parent_rows, BS, BS), jnp.float32)
    for child, (at, ok), target in zip(children, cols, row_targets):
        slabs = jnp.stack(
            [
                lax.dynamic_slice(child, (at[i], 0, 0), (1, rows, BS))[0]
                * ok[i].astype(jnp.float32)
                for i in range(panel_cols)
            ]
        ).reshape(panel_cols, child_rows, BS, BS)
        select = (target[None, :] == jnp.arange(parent_rows)[:, None]).astype(jnp.float32)
        west = west + jnp.einsum("pk,qkxy->qpxy", select, slabs, precision=exact)
    below = (jnp.arange(parent_rows) >= panel_rows).astype(jnp.float32)
    west = west * below[None, :, None, None]
    western = jnp.transpose(both_sides(west), (2, 3, 1, 0, 4)).reshape(parent_rows * BS, width)

    inverse = jnp.diag(1.0 / pivot_diag)
    for sweep in range(NS_STEPS):
        inverse = 2.0 * inverse - matmul(matmul(inverse, pivot), inverse)
    scaled_high, scaled_low = split(matmul(western, inverse))

    scalars = (*cols[0], *cols[1], *lines[0], *lines[1])
    result = update(
        panel_rows, panel_cols, scalars, first, second, scaled_high, scaled_low, northern, parent_cols
    )
    return result.reshape(1, parent_rows, 1, BS, parent_cols, 1, BS)


def on_device(contribution, *others):
    row_count = lax.axis_size("row")
    col_count = lax.axis_size("col")
    paired = (
        col_count == 2
        and row_count % 2 == 0
        and PANB % row_count == 0
        and (PANB // col_count) % 2 == 0
        and contribution.shape[4] % GROUP == 0
        and (PB // col_count) % GROUP == 0
    )
    chosen = on_device_paired if paired else on_device_general
    return chosen(contribution, *others)


def solution(mesh):
    placed = (
        P("leaf", None, "row", None, None, "col", None),
        P("leaf", None, "row", None, "col"),
        P("leaf", "row", None, "col", None),
        P(),
        P(),
        P(),
    )
    return jax.shard_map(
        on_device,
        mesh=mesh,
        in_specs=placed,
        out_specs=P("leaf", None, "row", None, None, "col", None),
        check_vma=False,
    )
```

```python
import functools

import jax
import jax.numpy as jnp
from jax import lax
from jax.experimental import pallas as pl
from jax.experimental.pallas import tpu as pltpu
from jax.sharding import PartitionSpec as P

BS = 128
CB = 40
PB = 64
PANB = 4
CPAN = 1024
NS_STEPS = 2


def partner(block, axis, stride):
    count = lax.axis_size(axis)
    route = []
    for low in range(count):
        high = low | 1 << stride
        if high != low and high < count:
            route += [(low, high), (high, low)]
    return lax.ppermute(block, axis, route)


def from_root(x, axis, root):
    mine = lax.axis_index(axis) == root
    return lax.psum(jnp.where(mine, x, jnp.zeros_like(x)), axis)


def matmul(first, second):
    return jnp.dot(
        first, second, precision=lax.Precision.HIGHEST, preferred_element_type=jnp.float32
    )


def on_device_general(contribution, panel_left, panel_right, block_masks, index_maps, pivot_diag):
    row_count = lax.axis_size("row")
    col_count = lax.axis_size("col")
    half_cols = col_count // 2
    leaf_index = lax.axis_index("leaf")
    row_index = lax.axis_index("row")
    col_index = lax.axis_index("col")
    child_side = col_index // half_cols
    group_index = col_index % half_cols
    child_rows = contribution.shape[1]
    child_cols = contribution.shape[4]
    parent_rows = PB // row_count
    parent_cols = PB // col_count
    width = PANB * BS
    cmat = contribution.reshape(child_rows * BS, child_cols * BS)
    gathered_right = lax.all_gather(panel_right, "row", axis=1, tiled=True)
    right = gathered_right.reshape(CPAN, child_cols * BS)
    gathered_left = lax.all_gather(panel_left, "col", axis=4, tiled=True)
    paired = gathered_left.reshape(child_rows * BS, CPAN, 2)
    first_child = paired[:, :, 0]
    second_child = paired[:, :, 1]
    left = jnp.where(child_side == 0, first_child, second_child)
    product = matmul(left, right)
    own_mask = block_masks[leaf_index, child_side]
    own_mask = own_mask.reshape(child_rows, row_count, CB)[:, row_index]
    own_mask = own_mask.reshape(child_rows, child_cols, half_cols)[:, :, group_index].astype(
        jnp.float32
    )
    schur = (cmat - product).reshape(child_rows, BS, child_cols, BS) * own_mask[:, None, :, None]
    own_map = index_maps[leaf_index, child_side]
    target = own_map.reshape(child_cols, half_cols)[:, group_index]
    stays = (target % col_count // half_cols == child_side).astype(jnp.float32)
    kept_here = schur * stays[None, None, :, None]
    leaving = schur * (1.0 - stays)[None, None, :, None]
    top_bit = col_count.bit_length() - 2
    arrived = partner(leaving, "col", top_bit)
    outgoing = jnp.where(child_side == 0, arrived, kept_here)
    staying = jnp.where(child_side == 0, kept_here, arrived)
    incoming = partner(outgoing, "leaf", 0)

    def assemble(piece, mapping):
        row_map = mapping.reshape(child_rows, row_count)[:, row_index] // row_count
        row_select = (row_map[None, :] == jnp.arange(parent_rows)[:, None]).astype(jnp.float32)
        col_map = mapping.reshape(child_cols, half_cols)[:, group_index]
        wanted = jnp.arange(parent_cols) * col_count + col_index
        col_select = (col_map[None, :] == wanted[:, None]).astype(jnp.float32)
        placed = jnp.einsum("pk,kxly->pxly", row_select, piece, precision=lax.Precision.HIGHEST)
        return jnp.einsum("pxly,ql->pxqy", placed, col_select, precision=lax.Precision.HIGHEST)

    first_map = index_maps[leaf_index, 0]
    second_map = index_maps[jnp.bitwise_xor(leaf_index, 1), 1]
    assembled = assemble(staying, first_map) + assemble(incoming, second_map)
    row_blocks = jnp.arange(parent_rows) * row_count + row_index
    col_blocks = jnp.arange(parent_cols) * col_count + col_index
    on_pivot = ((row_blocks[:, None] == col_blocks[None, :]) & (row_blocks[:, None] < PANB)).astype(
        jnp.float32
    )
    diag_rows = pivot_diag.reshape(PANB, BS)[jnp.clip(row_blocks, 0, PANB - 1)]
    identity = jnp.eye(BS, dtype=jnp.float32)
    assembled = assembled + on_pivot[:, None, :, None] * (
        diag_rows[:, :, None, None] * identity[None, :, None, :]
    )
    column_parts = []
    for block in range(PANB):
        owned = assembled[:, :, block // col_count, :]
        column_parts.append(from_root(owned, "col", block % col_count))
    western_raw = jnp.stack(column_parts, axis=2).reshape(parent_rows, BS, width)
    pieces_row = PANB // row_count
    north_raw = lax.all_gather(assembled[:pieces_row], "row", axis=0, tiled=True)
    north_raw = north_raw.reshape(row_count, pieces_row, BS, parent_cols * BS)
    north_raw = jnp.transpose(north_raw, (1, 0, 2, 3)).reshape(width, parent_cols * BS)
    pivot = lax.all_gather(western_raw[:pieces_row], "row", axis=0, tiled=True)
    pivot = jnp.transpose(pivot.reshape(row_count, pieces_row, BS, width), (1, 0, 2, 3)).reshape(
        width, width
    )
    inverse = jnp.diag(1.0 / pivot_diag)
    for sweep in range(NS_STEPS):
        inverse = 2.0 * inverse - matmul(matmul(inverse, pivot), inverse)
    western = (western_raw * (row_blocks >= PANB).astype(jnp.float32)[:, None, None]).reshape(
        parent_rows * BS, width
    )
    col_keep = jnp.repeat((col_blocks >= PANB).astype(jnp.float32), BS)
    northern = north_raw * col_keep[None, :]
    update = matmul(matmul(western, inverse), northern)
    result = assembled.reshape(parent_rows * BS, parent_cols * BS) - update
    keep_mask = ((row_blocks >= PANB)[:, None] & (col_blocks >= PANB)[None, :]).astype(jnp.float32)
    result = result.reshape(parent_rows, BS, parent_cols, BS) * keep_mask[:, None, :, None]
    return result.reshape(1, parent_rows, 1, BS, parent_cols, 1, BS)


GROUP = 8
VMEM_LIMIT = 60 * 1024 * 1024


def split(x):
    high = lax.reduce_precision(x, 8, 7)
    return high.astype(jnp.bfloat16), (x - high).astype(jnp.bfloat16)


def split_in_kernel(x):
    high = x.astype(jnp.bfloat16)
    return high, (x - high.astype(jnp.float32)).astype(jnp.bfloat16)


def dot3(a_high, a_low, b_high, b_low):
    dot = functools.partial(jnp.dot, preferred_element_type=jnp.float32)
    return dot(a_high, b_high) + (dot(a_high, b_low) + dot(a_low, b_high))


def whole(shape):
    return pl.BlockSpec(shape, lambda *_: (0,) * len(shape))


def schur_kernel(chunk, side_ref, mask_ref, lh_ref, ll_ref, r_ref, c_ref, own_ref, send_ref, rh, rl):
    side = side_ref[0]
    rows, depth = lh_ref.shape
    step = pl.program_id(0)
    r_flat = r_ref.reshape(depth * GROUP, BS)
    c_flat = c_ref.reshape(rows * GROUP, BS)

    @pl.when(step == 0)
    def _():
        for pair in range(GROUP // 2):
            right = jnp.concatenate(
                [
                    r_flat[pl.ds(q, depth, stride=GROUP), :]
                    for q in (2 * pair + side, 2 * pair + 1 - side)
                ],
                axis=1,
            )
            rh[pair], rl[pair] = split_in_kernel(right)

    for pair in range(GROUP // 2):
        product = dot3(lh_ref[...], ll_ref[...], rh[pair], rl[pair])
        for place, (q, out_ref) in enumerate(
            ((2 * pair + side, own_ref), (2 * pair + 1 - side, send_ref))
        ):
            c_part = c_flat[pl.ds(q, rows, stride=GROUP), :]
            value = c_part - product[:, place * BS : (place + 1) * BS]
            for block in range(rows // BS):
                keep = mask_ref[step * (rows // BS) + block, chunk * GROUP + q]
                lines = slice(block * BS, (block + 1) * BS)
                out_ref[pair, lines, :] = value[lines] * keep.astype(jnp.float32)


def schur_chunk(chunk, inside, side, mask, left_high, left_low, right, cmat):
    rows, depth = left_high.shape
    half = jax.ShapeDtypeStruct((GROUP // 2, rows, BS), jnp.float32)
    part = 2 * BS if rows % (2 * BS) == 0 else BS
    halves = pl.BlockSpec((GROUP // 2, part, BS), lambda i, *_: (0, i, 0))
    return pl.pallas_call(
        functools.partial(schur_kernel, chunk),
        out_shape=(half, half),
        grid_spec=pltpu.PrefetchScalarGridSpec(
            num_scalar_prefetch=2,
            grid=(rows // part,),
            in_specs=[
                pl.BlockSpec((part, depth), lambda i, *_: (i, 0)),
                pl.BlockSpec((part, depth), lambda i, *_: (i, 0)),
                pl.BlockSpec((depth, GROUP, BS), lambda i, *_: (0, inside, 0)),
                pl.BlockSpec((part, GROUP, BS), lambda i, *_: (i, chunk, 0)),
            ],
            out_specs=[halves, halves],
            scratch_shapes=[pltpu.VMEM((GROUP // 2, depth, 2 * BS), jnp.bfloat16)] * 2,
        ),
        compiler_params=pltpu.CompilerParams(vmem_limit_bytes=VMEM_LIMIT),
        cost_estimate=pl.CostEstimate(
            flops=6 * rows * depth * GROUP * BS,
            bytes_accessed=4 * (rows * depth + depth * GROUP * BS + 2 * rows * GROUP * BS),
            transcendentals=0,
        ),
        name="schur_chunk",
    )(side, mask, left_high, left_low, right, cmat)


def north_kernel(sizes, pieces, at0, ok0, at1, ok1, pivot_ref, first_ref, second_ref, diag_ref, *outs):
    parent_cols = sum(sizes)
    base = 0
    for size, out_ref in zip(sizes, outs):
        for piece in range(pieces):

            def body(place, carry, base=base, piece=piece, out_ref=out_ref):
                q = base + place
                out_ref[piece, place] = (
                    first_ref[piece, at0[q]] * ok0[q].astype(jnp.float32)
                    + second_ref[piece, at1[q]] * ok1[q].astype(jnp.float32)
                    + diag_ref[piece] * pivot_ref[piece * parent_cols + q].astype(jnp.float32)
                )
                return carry

            lax.fori_loop(0, size, body, 0)
        base += size


def north_strips(sizes, scalars, on_pivot, first, second, diag):
    pieces = first.shape[0]
    shapes = [(pieces, size, BS, BS) for size in sizes]
    return pl.pallas_call(
        functools.partial(north_kernel, sizes, pieces),
        out_shape=[jax.ShapeDtypeStruct(shape, jnp.float32) for shape in shapes],
        grid_spec=pltpu.PrefetchScalarGridSpec(
            num_scalar_prefetch=5,
            grid=(1,),
            in_specs=[whole(first.shape), whole(second.shape), whole(diag.shape)],
            out_specs=[whole(shape) for shape in shapes],
        ),
        compiler_params=pltpu.CompilerParams(vmem_limit_bytes=VMEM_LIMIT),
        name="north_strips",
    )(*scalars, on_pivot, first, second, diag)


def west_kernel(skip, col0, cok0, col1, cok1, row0, rok0, row1, rok1, first_ref, second_ref, out_ref):
    q = pl.program_id(0)

    def body(k, carry):
        total = jnp.zeros((BS, BS), jnp.float32)
        for ref, cok, row, rok in ((first_ref, cok0, row0, rok0), (second_ref, cok1, row1, rok1)):
            lines = pl.ds(pl.multiple_of(row[k] * BS, BS), BS)
            total = total + ref[0, lines, :] * (cok[q] * rok[k]).astype(jnp.float32)
        below = jnp.where(k >= skip, 1.0, 0.0).astype(jnp.float32)
        out_ref[0, pl.ds(pl.multiple_of(k * BS, BS), BS), :] = total * below
        return carry

    lax.fori_loop(0, out_ref.shape[1] // BS, body, 0)


def west_columns(skip, panel_cols, parent_rows, scalars, first, second):
    def slab(which):
        return pl.BlockSpec((1, first.shape[1], BS), lambda q, *pre: (pre[which][q], 0, 0))

    rows = parent_rows * BS
    return pl.pallas_call(
        functools.partial(west_kernel, skip),
        out_shape=jax.ShapeDtypeStruct((panel_cols, rows, BS), jnp.float32),
        grid_spec=pltpu.PrefetchScalarGridSpec(
            num_scalar_prefetch=8,
            grid=(panel_cols,),
            in_specs=[slab(0), slab(2)],
            out_specs=pl.BlockSpec((1, rows, BS), lambda q, *_: (q, 0, 0)),
        ),
        compiler_params=pltpu.CompilerParams(vmem_limit_bytes=VMEM_LIMIT),
        name="west_columns",
    )(*scalars, first, second)


def scale_kernel(mine_ref, other_ref, near_ref, far_ref, high_ref, low_ref):
    count = mine_ref.shape[0]
    panel = jnp.concatenate([ref[i] for ref in (mine_ref, other_ref) for i in range(count)], axis=1)
    middle = jnp.concatenate([ref[i] for ref in (near_ref, far_ref) for i in range(count)], axis=0)
    scaled = dot3(*split_in_kernel(panel), *split_in_kernel(middle))
    high_ref[...], low_ref[...] = split_in_kernel(scaled)


def scale(mine, other, near, far):
    count, rows, _ = mine.shape
    width = near.shape[2]
    part = 4 * BS if rows % (4 * BS) == 0 else BS
    block = pl.BlockSpec((count, part, BS), lambda i: (0, i, 0))
    out = pl.BlockSpec((part, width), lambda i: (i, 0))
    return pl.pallas_call(
        scale_kernel,
        out_shape=[jax.ShapeDtypeStruct((rows, width), jnp.bfloat16)] * 2,
        grid=(rows // part,),
        in_specs=[block, block, whole(near.shape), whole(far.shape)],
        out_specs=[out, out],
        compiler_params=pltpu.CompilerParams(vmem_limit_bytes=VMEM_LIMIT),
        name="scaled_panel",
    )(mine, other, near, far)


def update_kernel(first_keep, panel_cols, row_step, base, first_col, first_colok, second_col, second_colok, first_row, first_rowok, second_row, second_rowok, *refs):
    first = refs[:GROUP]
    second = refs[GROUP : 2 * GROUP]
    wh_ref, wl_ref = refs[2 * GROUP : 2 * GROUP + 2]
    v_refs = refs[2 * GROUP + 2 : 2 * GROUP + 2 + GROUP // 2]
    out_ref = refs[-1]
    rows, width = wh_ref.shape
    out_flat = out_ref.reshape(rows * GROUP, BS)
    group = base + pl.program_id(0)
    blocks = row_step // BS
    for pair in range(GROUP // 2):
        v_ref = v_refs[pair]
        v = jnp.concatenate([v_ref[:, i].reshape(width, BS) for i in range(2)], axis=1)
        v_high, v_low = split_in_kernel(v)

        def body(step, carry):
            lines = pl.ds(pl.multiple_of(step * row_step, row_step), row_step)
            product = dot3(wh_ref[lines, :], wl_ref[lines, :], v_high, v_low)
            for block in range(blocks):
                k = step * blocks + block
                for i in range(2):
                    place = 2 * pair + i
                    q = group * GROUP + place
                    keep = jnp.where((k >= first_keep) & (q >= panel_cols), 1.0, 0.0).astype(
                        jnp.float32
                    )
                    total = -product[block * BS : (block + 1) * BS, i * BS : (i + 1) * BS]
                    for slabs, col_ok, row_at, row_ok in (
                        (first, first_colok, first_row, first_rowok),
                        (second, second_colok, second_row, second_rowok),
                    ):
                        use = (col_ok[q] * row_ok[k]).astype(jnp.float32)
                        from_row = pl.multiple_of(row_at[k] * BS, BS)
                        total = total + slabs[place][0, pl.ds(from_row, BS), :] * use
                    out_flat[pl.ds(k * (BS * GROUP) + place, BS, stride=GROUP), :] = total * keep
            return carry

        lax.fori_loop(0, rows // row_step, body, 0)


def update(first_keep, panel_cols, scalars, first, second, w_high, w_low, northern, parent_cols, base, front):
    rows, width = w_high.shape
    child_rows = first.shape[1]
    pieces = northern.shape[0]
    row_step = 4 * BS if rows % (4 * BS) == 0 else BS

    held = () if front is None else (front,)
    inputs = (
        [first] * GROUP + [second] * GROUP + [w_high, w_low] + [northern] * (GROUP // 2) + [*held]
    )

    def slab(which, place):
        def at(g, *prefetched):
            return prefetched[which][(base + g) * GROUP + place], 0, 0

        return pl.BlockSpec((1, child_rows, BS), at)

    def north(pair):
        def at(g, *_):
            return 0, g * (GROUP // 2) + pair, 0, 0

        return pl.BlockSpec((pieces, 2, BS, BS), at)

    panel = pl.BlockSpec((rows, width), lambda g, *_: (0, 0), pipeline_mode=pl.Buffered(1))
    return pl.pallas_call(
        functools.partial(update_kernel, first_keep, panel_cols, row_step, base),
        out_shape=jax.ShapeDtypeStruct((rows, parent_cols, BS), jnp.float32),
        grid_spec=pltpu.PrefetchScalarGridSpec(
            num_scalar_prefetch=8,
            grid=(northern.shape[1] // GROUP,),
            in_specs=[slab(0, i) for i in range(GROUP)]
            + [slab(2, i) for i in range(GROUP)]
            + [panel, panel]
            + [north(i) for i in range(GROUP // 2)]
            + [pl.BlockSpec(memory_space=pl.ANY)] * len(held),
            out_specs=pl.BlockSpec((rows, GROUP, BS), lambda g, *_: (0, base + g, 0)),
        ),
        compiler_params=pltpu.CompilerParams(vmem_limit_bytes=VMEM_LIMIT),
        cost_estimate=pl.CostEstimate(
            flops=6 * rows * width * northern.shape[1] * BS,
            bytes_accessed=4 * (2 * child_rows + rows + width) * northern.shape[1] * BS,
            transcendentals=0,
        ),
        name="front_update",
        input_output_aliases={8 + len(inputs) - 1: 0} if held else {},
    )(*scalars, *inputs)


def inverse_map(targets, count):
    hits = targets[None, :] == jnp.arange(count, dtype=jnp.int32)[:, None]
    return jnp.argmax(hits, axis=1).astype(jnp.int32), jnp.any(hits, axis=1).astype(jnp.int32)


def on_device_paired(contribution, panel_left, panel_right, block_masks, index_maps, pivot_diag):
    row_count = lax.axis_size("row")
    col_count = lax.axis_size("col")
    leaf_index = lax.axis_index("leaf")
    row_index = lax.axis_index("row")
    side = lax.axis_index("col")
    child_rows = contribution.shape[1]
    child_cols = contribution.shape[4]
    blocks = child_rows * row_count
    rows = child_rows * BS
    parent_rows = PB // row_count
    parent_cols = PB // col_count
    width = PANB * BS
    panel_rows = PANB // row_count
    panel_cols = PANB // col_count

    cmat = contribution.reshape(rows, child_cols, BS)
    right_local = panel_right.reshape(panel_right.shape[1], child_cols, BS)
    depth = right_local.shape[0] * row_count

    def gather_right(chunk, *after):
        piece = right_local[:, chunk * GROUP : (chunk + 1) * GROUP]
        if after:
            piece = lax.optimization_barrier((piece, *after))[0]
        if chunk % 2 == 0:
            return lax.all_gather(piece, "row", axis=0, tiled=True)
        whole_piece = lax.all_gather(piece[None], "row", axis=1, tiled=True)
        return whole_piece.reshape(depth, GROUP, BS)

    local_left = panel_left.reshape(rows, panel_left.shape[4])
    local_depth = local_left.shape[1] // 2
    line = jnp.arange(2 * local_depth)[:, None]
    pick = 2 * jnp.arange(local_depth)[None, :]
    parted = [
        jnp.dot(
            local_left, (line == pick + offset).astype(jnp.float32), precision=lax.Precision.HIGH
        )
        for offset in (side, 1 - side)
    ]
    kept, given = parted
    taken = partner(given, "col", 0)
    left = jnp.where(
        side == 0,
        jnp.concatenate([kept, taken], axis=1),
        jnp.concatenate([taken, kept], axis=1),
    )
    left_high, left_low = split(left)

    mask = block_masks[leaf_index, side].reshape(child_rows, row_count, blocks)[:, row_index]
    side_arg = side.astype(jnp.int32).reshape(1)
    maps = (index_maps[leaf_index, 0], index_maps[jnp.bitwise_xor(leaf_index, 1), 1])
    row_targets = [
        m.reshape(child_rows, row_count)[:, row_index].astype(jnp.int32) // row_count for m in maps
    ]
    col_targets = [
        m.reshape(child_cols // 2, 2)[:, side].astype(jnp.int32) // col_count for m in maps
    ]
    cols = [inverse_map(t, parent_cols) for t in col_targets]
    lines = [inverse_map(t, parent_rows) for t in row_targets]
    own_map = index_maps[leaf_index, side].reshape(child_rows, row_count)[:, row_index]
    own_at, own_ok = inverse_map(own_map.astype(jnp.int32) // row_count, parent_rows)

    def strip(block):
        return jnp.stack(
            [
                lax.dynamic_slice(block, (0, own_at[i] * BS, 0), (GROUP // 2, BS, BS))
                * own_ok[i].astype(jnp.float32)
                for i in range(panel_rows)
            ]
        )

    def crossed(own, sent):
        got = partner(sent, "col", 0)
        return jnp.where(side == 0, own, got), jnp.where(side == 0, got, own)

    first = jnp.zeros((child_cols // 2, rows, BS), jnp.float32)
    second = jnp.zeros((child_cols // 2, rows, BS), jnp.float32)
    strips = ([], [])
    chunks = child_cols // GROUP
    gathered = [gather_right(chunk) for chunk in range(min(2, chunks))]
    done = []
    leaving_all = []
    for chunk in range(chunks):
        current = gathered[chunk]
        after = (leaving_all[chunk - 1] + done[chunk - 1]) if chunk else [left_high, left_low]
        if chunk + 2 < chunks:
            gathered.append(gather_right(chunk + 2, current, *after))
        elif chunk + 1 == chunks and chunk > 1:
            after = leaving_all[chunk - 1] + done[chunk - 2] + [strips[1][chunk - 1]]
            current = lax.optimization_barrier((current, *after))[0]
        own, sent = schur_chunk(chunk, 0, side_arg, mask, left_high, left_low, current, cmat)
        kept_strip, leaving_strip = crossed(strip(own), strip(sent))
        strips[0].append(kept_strip)
        strips[1].append(partner(leaving_strip, "leaf", 0))
        kept, leaving = crossed(own, sent)
        incoming = partner(leaving, "leaf", 0)
        at = chunk * (GROUP // 2)
        first = lax.dynamic_update_slice(first, kept, (at, 0, 0))
        second = lax.dynamic_update_slice(second, incoming, (at, 0, 0))
        leaving_all.append([leaving, leaving_strip])
        done.append([incoming, strips[1][-1]])

    identity = jnp.eye(BS, dtype=jnp.float32)
    diag = pivot_diag.reshape(PANB, BS)
    col_blocks = jnp.arange(parent_cols) * col_count + side
    panel_blocks = jnp.arange(panel_rows) * row_count + row_index
    diag_blocks = diag[panel_blocks][:, :, None] * identity[None]
    on_pivot = (panel_blocks[:, None] == col_blocks[None, :]).astype(jnp.int32).reshape(-1)
    groups = parent_cols // GROUP
    widths = (1, groups - 2, 1) if groups > 2 else (1,) * groups
    north = north_strips(
        tuple(w * GROUP for w in widths),
        (*cols[0], *cols[1]),
        on_pivot,
        jnp.concatenate(strips[0], axis=1),
        jnp.concatenate(strips[1], axis=1),
        diag_blocks,
    )
    northern = []
    for piece in north:
        if northern:
            before = [incoming[0] for incoming in done[-2:-1]] if len(northern) == 1 else []
            piece = lax.optimization_barrier((piece, northern[-1], *before))[0]
        northern.append(lax.all_gather(piece, "row", axis=1))
    northern = [piece.reshape(PANB, -1, BS, BS) for piece in northern]

    corner = northern[0][:, :panel_cols]
    far_corner = partner(corner, "col", 0)
    both = jnp.where(
        side == 0, jnp.stack([corner, far_corner]), jnp.stack([far_corner, corner])
    )
    pivot = jnp.transpose(both, (1, 3, 2, 0, 4)).reshape(width, width)
    inverse = jnp.diag(1.0 / pivot_diag)
    for sweep in range(NS_STEPS):
        inverse = 2.0 * inverse - matmul(matmul(inverse, pivot), inverse)
    bands = inverse.reshape(panel_cols, 2, BS, width)
    near = jnp.where(side == 0, bands[:, 0], bands[:, 1])
    far = jnp.where(side == 0, bands[:, 1], bands[:, 0])

    scalars = (*cols[0], *cols[1], *lines[0], *lines[1])
    west = west_columns(panel_rows, panel_cols, parent_rows, scalars, first, second)
    scaled_high, scaled_low = scale(west, partner(west, "col", 0), near, far)

    front = None
    base = 0
    for size, piece in zip(widths, northern):
        front = update(
            panel_rows,
            panel_cols,
            scalars,
            first,
            second,
            scaled_high,
            scaled_low,
            piece,
            parent_cols,
            base,
            front,
        )
        base += size
    return front.reshape(1, parent_rows, 1, BS, parent_cols, 1, BS)


def on_device(contribution, *others):
    row_count = lax.axis_size("row")
    col_count = lax.axis_size("col")
    paired = (
        col_count == 2
        and row_count % 2 == 0
        and PANB % row_count == 0
        and (PANB // col_count) % 2 == 0
        and contribution.shape[4] % GROUP == 0
        and (PB // col_count) % GROUP == 0
    )
    chosen = on_device_paired if paired else on_device_general
    return chosen(contribution, *others)


def solution(mesh):
    placed = (
        P("leaf", None, "row", None, None, "col", None),
        P("leaf", None, "row", None, "col"),
        P("leaf", "row", None, "col", None),
        P(),
        P(),
        P(),
    )
    return jax.shard_map(
        on_device,
        mesh=mesh,
        in_specs=placed,
        out_specs=P("leaf", None, "row", None, None, "col", None),
        check_vma=False,
    )
```
